32 devices in a mesh: section: 4 (over z), seq: 8 (over y, x, core).
Axes of the slice: x: 2, y: 2, z: 4, core: 2. Of those that a mesh axis runs over, the one named last changes fastest.
Arguments:
- inputs: bfloat16 [512, 4096], P('seq'), may hold values from -6 to 6
- gains: float32 [4, 4096], P('section'), may hold values from 0.25 to 1.75
- weights: bfloat16 [4, 4096, 4096], P('section', None, 'seq'), may hold values from -0.125 to 0.125
- keep: int32 [4, 64, 64], P('section', None, 'seq'), may hold values 0 or 1
- cotangent: bfloat16 [512, 4096], P('seq'), may hold values from -6 to 6
Outputs:
- layer_outputs: bfloat16 [4, 512, 4096], P('section', 'seq')
- layer_grads: bfloat16 [4, 512, 4096], P('section', 'seq')
- weight_grads: bfloat16 [4, 4096, 4096], P('section', None, 'seq')
- gain_grads: float32 [4, 4096], P('section', 'seq')
The draws below stay inside these ranges and needn't reach their ends.
Inputs may be any that keep to these rules, and one draw needn't show every extreme that they name: `keep`: 1 keeps a 64 x 64 block of the projection, 0 prunes it.
All inputs are finite; a program needn't handle non-finite values.
Results may differ from the reference program's by a relative error of at most 0.018.
Values may be sent and summed in bfloat16 or wider, within the bound.
A program may use at most 64 MiB of HBM per device.

```python
import jax
import jax.numpy as jnp
from jax import lax

D = 4096
BLOCK = 64
LAYERS = 4
TOKENS = 512
N_SEQ = 8


def set_ends(values, stream_key, low, high):
    extent = values.shape
    place = [jax.random.randint(jax.random.fold_in(stream_key, axis), (), 0, extent[axis]) for axis in range(len(extent))]
    values = values.at[tuple(place)].set(low)
    longest = extent.index(max(extent))
    place[longest] = (place[longest] + 1) % extent[longest]
    return values.at[tuple(place)].set(high)


def steps_of(own_key, dims, cuts, least, high):
    factor_of, own = 1.0, jax.random.fold_in(own_key, 6)
    for position, shards_of in cuts:
        heights = jnp.exp(jax.random.uniform(jax.random.fold_in(own, position), (shards_of,), jnp.float32, least / len(cuts), high / len(cuts)))
        factor_of = factor_of * jnp.repeat(heights, dims[position] // shards_of).reshape([-1 if axis == position else 1 for axis in range(len(dims))])
    return factor_of


def centred(rng, dims, deviation, limit, pieces=(), kind=jnp.bfloat16):
    entries = jax.random.normal(rng, dims, jnp.float32) * deviation
    if len(pieces) > 0:
        entries = steps_of(rng, dims, pieces, -0.22, 0.18) * entries
    return jnp.clip(entries, min=-limit, max=limit).astype(kind)


def setup_inputs(seed: int = 0) -> dict:
    streams_of = jax.random.split(jax.random.key(seed), 6)
    inputs = centred(streams_of[0], (TOKENS, D), 1.0, 6.0, ((0, 8),))
    gains = jnp.clip(1.0 + 0.15 * jax.random.normal(streams_of[1], (LAYERS, D), jnp.float32), 0.25, 1.75)
    weights = centred(streams_of[2], (LAYERS, D, D), (D // 2) ** -0.5, 0.125, ((0, 4), (2, 8)))
    keep = set_ends((jax.random.randint(streams_of[3], (LAYERS, D // BLOCK, D // BLOCK), 0, 2) < 1).astype(jnp.int32), jax.random.fold_in(streams_of[3], 1), 0, 1)
    cotangent = centred(streams_of[4], (TOKENS, D), 1.0, 6.0, ((0, 8),))
    return {"inputs": inputs, "gains": gains, "weights": weights, "keep": keep, "cotangent": cotangent}


epsilon = 1e-05

def expand_keep(keep_layer):
    return jnp.repeat(jnp.repeat(keep_layer, BLOCK, axis=0), BLOCK, axis=1).astype(jnp.bfloat16)

def normalize(layer_in, gain_row):
    x_float = layer_in.astype(jnp.float32)
    inverse_rms = lax.rsqrt(lax.optimization_barrier(jnp.mean(x_float * x_float, axis=1, keepdims=True)) + epsilon)
    normed = (x_float * inverse_rms * gain_row[None, :]).astype(jnp.bfloat16)
    return (x_float, inverse_rms, normed)

def reference(inputs, gains, weights, keep, cotangent):
    layer_in = inputs
    input_list = []
    output_list = []
    for layer_index in range(LAYERS):
        masked = weights[layer_index] * expand_keep(keep[layer_index])
        x_float, inverse_rms, normed = normalize(layer_in, gains[layer_index])
        mixed = jnp.dot(normed, masked, preferred_element_type=jnp.float32).astype(jnp.bfloat16)
        result = (x_float + mixed.astype(jnp.float32)).astype(jnp.bfloat16)
        input_list.append(layer_in)
        output_list.append(result)
        layer_in = result
    col_width = D // N_SEQ
    upstream = cotangent
    grad_list = []
    wgrad_list = []
    gain_list = []
    for layer_index in range(LAYERS - 1, -1, -1):
        keep_mask = expand_keep(keep[layer_index])
        masked = weights[layer_index] * keep_mask
        x_float, inverse_rms, normed = normalize(input_list[layer_index], gains[layer_index])
        wgrad = lax.dot_general(normed, upstream, (((0,), (0,)), ((), ())), preferred_element_type=jnp.float32)
        wgrad_list.append((wgrad * keep_mask.astype(jnp.float32)).astype(jnp.bfloat16))
        normgrad = jnp.zeros(upstream.shape, jnp.float32)
        for part_index in range(N_SEQ):
            lower = part_index * col_width
            partial_sum = lax.dot_general(upstream[:, lower:lower + col_width], masked[:, lower:lower + col_width], (((1,), (1,)), ((), ())), preferred_element_type=jnp.float32)
            rounded = lax.optimization_barrier(partial_sum.astype(jnp.bfloat16))
            normgrad = normgrad + rounded.astype(jnp.float32)
        scaled = gains[layer_index][None, :] * normgrad
        inner = lax.optimization_barrier(jnp.sum(x_float * scaled, axis=1, keepdims=True)) / D
        layer_grad = (upstream.astype(jnp.float32) + inverse_rms * scaled - x_float * inverse_rms * inverse_rms * inverse_rms * inner).astype(jnp.bfloat16)
        gain_list.append(lax.optimization_barrier(jnp.sum(normgrad * x_float * inverse_rms, axis=0)))
        grad_list.append(layer_grad)
        upstream = layer_grad
    grad_list = grad_list[::-1]
    wgrad_list = wgrad_list[::-1]
    gain_list = gain_list[::-1]
    return (jnp.stack(output_list), jnp.stack(grad_list), jnp.stack(wgrad_list), jnp.stack(gain_list))
```

```python
import functools

import jax
import jax.numpy as jnp
from jax import lax
from jax.experimental import pallas as pl
from jax.experimental.pallas import tpu as pltpu
from jax.sharding import PartitionSpec as P

EPS = 1e-05
ROWS = 16
F32 = jnp.float32
BF16 = jnp.bfloat16


def dot(a, b, dims):
    return lax.dot_general(a, b, (dims, ((), ())), preferred_element_type=F32)


def to_row(column, rows):
    n = column.shape[0]
    return jnp.transpose(jnp.broadcast_to(column, (n, 128)))[:rows]


def to_col(row):
    n = row.shape[1]
    return jnp.transpose(jnp.broadcast_to(row, (128, n)))[:, :1]


def kernel(
    L, S, M, block,
    x_ref, gain_ref, w_ref, keep_ref, cot_ref,
    lo_ref, lg_ref, wg_ref, gg_ref,
    A, wp, raw, inv_ref, zout, g, zg, gs, tot, psend, prec, qsend, qrec, nsend, nrec, ggs, ggr,
    in_sem, cot_sem, ag_sem, lo2_sem, n_sem, p_sem, q_sem, lg_sem, gg_sem, zf_sem, lo_sem, zb_sem,
):
    r = x_ref.shape[1]
    D = w_ref.shape[0]
    C = w_ref.shape[1]
    MB = S * r
    H = S // 2
    sec = lax.axis_index("section")
    me = lax.axis_index("seq")
    pair = me // 2
    par = me % 2
    partner = pair * 2 + 1 - par
    is_first = sec == 0
    is_last = sec == L - 1

    def col(i):
        return pl.ds(pl.multiple_of(i * C, C), C)

    def rows(i):
        return pl.ds(pl.multiple_of(i * r, r), r)

    def to(j):
        return (me + j) % S

    def fr(j):
        return (me + S - j) % S

    def mate_to(j):
        return ((pair + j) % H) * 2 + par

    def mate_fr(j):
        return ((pair + H - j) % H) * 2 + par

    def cp(src, dst, sem, idx, dev, section=None):
        return pltpu.make_async_remote_copy(
            src_ref=src,
            dst_ref=dst,
            send_sem=sem.at[(0,) + idx],
            recv_sem=sem.at[(1,) + idx],
            device_id=(sec if section is None else section, dev),
            device_id_type=pl.DeviceIdType.MESH,
        )

    def same(ref, sem, idx, dev, section=None):
        return cp(ref, ref, sem, idx, dev, section)

    def in_tx(m, j):
        d = to(j)
        return cp(x_ref.at[m, :, col(d)], A.at[m, rows(me), col(d)], in_sem, (m, j), d)

    def in_rx(m, j):
        f = fr(j)
        return same(A.at[m, rows(f), col(me)], in_sem, (m, j), f)

    def cot_tx(m, j):
        d = to(j)
        return cp(cot_ref.at[m, :, col(d)], g.at[m, rows(me), :], cot_sem, (m, j), d)

    def cot_rx(m, j):
        f = fr(j)
        return same(g.at[m, rows(f), :], cot_sem, (m, j), f)

    def ag_tx(m, j):
        return same(A.at[m, :, col(me)], ag_sem, (m, j), mate_to(j))

    def ag_rx(m, j):
        f = mate_fr(j)
        return same(A.at[m, :, col(f)], ag_sem, (m, j), f)

    def ag_ptx(m):
        return same(A.at[m, :, col(me)], ag_sem, (m, 0), partner)

    def ag_prx(m):
        return same(A.at[m, :, col(partner)], ag_sem, (m, 0), partner)

    def ag_ftx(m, j):
        return same(A.at[m, :, col(mate_fr(j))], ag_sem, (m, H + j), partner)

    def ag_frx(m, j):
        b = mate_fr(j) + 1 - 2 * par
        return same(A.at[m, :, col(b)], ag_sem, (m, H + j), partner)

    def zf_tx(m):
        return cp(zout.at[m], A.at[m, :, col(me)], zf_sem, (m,), me, sec + 1)

    def zf_rx(m):
        return same(A.at[m, :, col(me)], zf_sem, (m,), me, sec - 1)

    def lo_tx(m):
        return cp(A.at[m, rows(me), :], lo_ref.at[m], lo_sem, (m,), me, sec - 1)

    def lo_rx(m):
        return same(lo_ref.at[m], lo_sem, (m,), me, sec + 1)

    def lo2_tx(m, j):
        d = to(j)
        return cp(zout.at[m, rows(d), :], lo_ref.at[m, :, col(me)], lo2_sem, (m, j), d)

    def lo2_rx(m, j):
        f = fr(j)
        return same(lo_ref.at[m, :, col(f)], lo2_sem, (m, j), f)

    def n_tx(m, j):
        return cp(nsend.at[m], nrec.at[m, j], n_sem, (m, j), to(j))

    def n_rx(m, j):
        return same(nrec.at[m, j], n_sem, (m, j), fr(j))

    def p_tx(m, j):
        return cp(psend.at[m, j], prec.at[m, j], p_sem, (m, j), partner)

    def p_rx(m, j):
        return same(prec.at[m, j], p_sem, (m, j), partner)

    def q_tx(m, j):
        return cp(qsend.at[m, j], qrec.at[m, j], q_sem, (m, j), mate_to(j))

    def q_rx(m, j):
        return same(qrec.at[m, j], q_sem, (m, j), mate_fr(j))

    def zb_tx(m):
        return cp(zg.at[m], g.at[m], zb_sem, (m,), me, sec - 1)

    def zb_rx(m):
        return same(g.at[m], zb_sem, (m,), me, sec + 1)

    def lg_tx(m, j):
        d = to(j)
        return cp(zg.at[m, rows(d), :], lg_ref.at[m, :, col(me)], lg_sem, (m, j), d)

    def lg_rx(m, j):
        f = fr(j)
        return same(lg_ref.at[m, :, col(f)], lg_sem, (m, j), f)

    def gg_tx(j):
        d = to(j)
        return cp(ggs.at[d], ggr.at[j], gg_sem, (j,), d)

    def gg_rx(j):
        return same(ggr.at[j], gg_sem, (j,), fr(j))

    others = range(1, S)
    mates = range(1, H)

    barrier = pltpu.get_barrier_semaphore()

    def greet(section, seq):
        pl.semaphore_signal(
            barrier, inc=1, device_id=(section, seq), device_id_type=pl.DeviceIdType.MESH
        )

    for j in others:
        greet(sec, to(j))

    @pl.when(sec > 0)
    def _():
        greet(sec - 1, me)

    @pl.when(sec < L - 1)
    def _():
        greet(sec + 1, me)

    neighbours = jnp.minimum(sec, 1) + jnp.minimum(L - 1 - sec, 1)
    pl.semaphore_wait(barrier, S - 1 + neighbours)

    @pl.when(is_first)
    def _():
        @pl.loop(0, M)
        def _(m):
            for j in others:
                in_tx(m, j).start()
            A[m, rows(me), col(me)] = x_ref[m, :, col(me)]

    @pl.when(is_last)
    def _():
        @pl.loop(0, M)
        def _(m):
            for j in others:
                cot_tx(m, j).start()
            g[m, rows(me), :] = cot_ref[m, :, col(me)]

    def keep_of(b):
        return jnp.broadcast_to(keep_ref[b][:, None, :], (C // block, block, C)).reshape(C, C)

    @pl.loop(0, S)
    def _(b):
        gain = to_col(gain_ref[:, col(b)])
        wp[col(b), :] = (w_ref[col(b), :].astype(F32) * gain * keep_of(b)).astype(BF16)

    def gather_start(m):
        for j in mates:
            ag_tx(m, j).start()
        ag_ptx(m).start()

    @pl.when(is_first)
    def _():
        @pl.loop(0, M)
        def _(m):
            for j in others:
                in_rx(m, j).wait_recv()
            gather_start(m)

    @pl.loop(0, M)
    def _(m):
        @pl.when(sec > 0)
        def _():
            zf_rx(m).wait_recv()
            gather_start(m)

        for j in mates:
            ag_rx(m, j).wait_recv()
            ag_ftx(m, j).start()
        ag_prx(m).wait_recv()
        for j in mates:
            ag_frx(m, j).wait_recv()

        @pl.when(sec > 0)
        def _():
            lo_tx(m).start()

        acc = jnp.zeros((MB, C), F32)
        squares = jnp.zeros((MB, 1), F32)
        for b in range(S):
            part = A[m, :, b * C:(b + 1) * C]
            acc = acc + dot(part, wp[b * C:(b + 1) * C, :], ((1,), (0,)))
            wide = part.astype(F32)
            squares = squares + jnp.sum(wide * wide, axis=1, keepdims=True)
        inv = lax.rsqrt(squares / D + EPS)
        raw[m] = acc
        inv_ref[m] = jnp.broadcast_to(inv, (MB, 128))
        zout[m] = (A[m, :, col(me)].astype(F32) + inv * acc).astype(BF16)

        @pl.when(sec < L - 1)
        def _():
            zf_tx(m).start()

        @pl.when(is_last)
        def _():
            for j in others:
                lo2_tx(m, j).start()
            lo_ref[m, :, col(me)] = zout[m, rows(me), :]

    def weight_grads():
        @pl.loop(0, S)
        def _(b):
            left = A[:, :, col(b)].reshape(M * MB, C)
            right = gs[...].reshape(M * MB, C)
            u = dot(left, right, ((0,), (0,))) * keep_of(b)
            wg_ref[col(b), :] = (u * to_col(gain_ref[:, col(b)])).astype(BF16)
            total = jnp.sum(u * w_ref[col(b), :].astype(F32), axis=1, keepdims=True)
            ggs[b] = to_row(total, 8)

        for j in others:
            gg_tx(j).start()

    @pl.loop(0, M)
    def _(m):
        @pl.when(is_last)
        def _():
            for j in others:
                cot_rx(m, j).wait_recv()

        @pl.when(sec < L - 1)
        def _():
            zb_rx(m).wait_recv()

        def partial_of(b):
            return dot(g[m], wp[col(b), :], ((1,), (1,)))

        order = list(mates) + [0]
        for j in order:
            psend[m, j] = partial_of(((pair + j) % H) * 2 + 1 - par).astype(BF16)
            p_tx(m, j).start()
        inv = inv_ref[m][:, :1]
        gv = g[m].astype(F32)
        nsend[m] = to_row(jnp.sum(gv * raw[m], axis=1, keepdims=True), 8)
        for j in others:
            n_tx(m, j).start()
        gs[m] = (gv * inv).astype(BF16)
        for j in mates:
            mine = partial_of(mate_to(j))
            p_rx(m, j).wait_recv()
            qsend[m, j] = (mine + prec[m, j].astype(F32)).astype(BF16)
            q_tx(m, j).start()
        tot[...] = partial_of(me)

        @pl.when(m == M - 1)
        def _():
            weight_grads()

        p_rx(m, 0).wait_recv()
        for j in mates:
            q_rx(m, j).wait_recv()
        for j in others:
            n_rx(m, j).wait_recv()
        scaled = tot[...] + prec[m, 0].astype(F32)
        for j in mates:
            scaled = scaled + qrec[m, j].astype(F32)
        sums = nsend[m]
        for j in others:
            sums = sums + nrec[m, j]
        inner = to_col(sums[:1]) / D
        grad = (
            g[m].astype(F32)
            + inv * scaled
            - A[m, :, col(me)].astype(F32) * (inv * inv * inv * inner)
        )
        zg[m] = grad.astype(BF16)

        @pl.when(sec > 0)
        def _():
            zb_tx(m).start()

        for j in others:
            lg_tx(m, j).start()
        lg_ref[m, :, col(me)] = zg[m, rows(me), :]

    for j in others:
        gg_rx(j).wait_recv()
    sums = ggs[me]
    for j in others:
        sums = sums + ggr[j]
    gg_ref[...] = sums[:1]

    for j in others:
        gg_tx(j).wait_send()

    @pl.loop(0, M)
    def _(m):
        @pl.when(is_first)
        def _():
            for j in others:
                in_tx(m, j).wait_send()

        @pl.when(is_last)
        def _():
            for j in others:
                cot_tx(m, j).wait_send()
                lo2_tx(m, j).wait_send()
                lo2_rx(m, j).wait_recv()

        @pl.when(sec < L - 1)
        def _():
            zf_tx(m).wait_send()
            lo_rx(m).wait_recv()

        @pl.when(sec > 0)
        def _():
            lo_tx(m).wait_send()
            zb_tx(m).wait_send()

        for j in mates:
            ag_tx(m, j).wait_send()
            ag_ftx(m, j).wait_send()
            q_tx(m, j).wait_send()
        ag_ptx(m).wait_send()
        for j in range(H):
            p_tx(m, j).wait_send()
        for j in others:
            n_tx(m, j).wait_send()
            lg_tx(m, j).wait_send()
            lg_rx(m, j).wait_recv()


def local(L, S, inputs, gains, weights, keep, cotangent):
    rows_dev, D = inputs.shape
    C = weights.shape[2]
    r = ROWS
    M = rows_dev // r
    MB = S * r
    H = S // 2
    block = D // keep.shape[1]
    keep_cols = jnp.repeat(keep[0].astype(F32), block, axis=1).reshape(S, C // block, C)
    vmem = pl.BlockSpec(memory_space=pltpu.VMEM)
    dma = pltpu.SemaphoreType.DMA
    lo, lg, wg, gg = pl.pallas_call(
        functools.partial(kernel, L, S, M, block),
        out_shape=(
            jax.ShapeDtypeStruct((M, r, D), BF16),
            jax.ShapeDtypeStruct((M, r, D), BF16),
            jax.ShapeDtypeStruct((D, C), BF16),
            jax.ShapeDtypeStruct((1, C), F32),
        ),
        in_specs=[vmem] * 5,
        out_specs=(vmem,) * 4,
        scratch_shapes=[
            pltpu.VMEM((M, MB, D), BF16),
            pltpu.VMEM((D, C), BF16),
            pltpu.VMEM((M, MB, C), F32),
            pltpu.VMEM((M, MB, 128), F32),
            pltpu.VMEM((M, MB, C), BF16),
            pltpu.VMEM((M, MB, C), BF16),
            pltpu.VMEM((M, MB, C), BF16),
            pltpu.VMEM((M, MB, C), BF16),
            pltpu.VMEM((MB, C), F32),
            pltpu.VMEM((M, H, MB, C), BF16),
            pltpu.VMEM((M, H, MB, C), BF16),
            pltpu.VMEM((M, H, MB, C), BF16),
            pltpu.VMEM((M, H, MB, C), BF16),
            pltpu.VMEM((M, 8, MB), F32),
            pltpu.VMEM((M, S, 8, MB), F32),
            pltpu.VMEM((S, 8, C), F32),
            pltpu.VMEM((S, 8, C), F32),
            dma((2, M, S)),
            dma((2, M, S)),
            dma((2, M, S)),
            dma((2, M, S)),
            dma((2, M, S)),
            dma((2, M, H)),
            dma((2, M, H)),
            dma((2, M, S)),
            dma((2, S)),
            dma((2, M)),
            dma((2, M)),
            dma((2, M)),
        ],
        compiler_params=pltpu.CompilerParams(
            collective_id=0, has_side_effects=True, vmem_limit_bytes=60 * 1024 * 1024
        ),
        cost_estimate=pl.CostEstimate(
            flops=6 * M * MB * D * C, bytes_accessed=12 * D * C, transcendentals=0
        ),
    )(
        inputs.reshape(M, r, D),
        gains,
        weights[0],
        keep_cols,
        cotangent.reshape(M, r, D),
    )
    return (
        lo.reshape(1, rows_dev, D),
        lg.reshape(1, rows_dev, D),
        wg[None],
        gg,
    )


def solution(mesh):
    placed = (
        P("seq", None),
        P("section", None),
        P("section", None, "seq"),
        P("section", None, "seq"),
        P("seq", None),
    )
    return jax.shard_map(
        functools.partial(local, mesh.shape["section"], mesh.shape["seq"]),
        mesh=mesh,
        in_specs=placed,
        out_specs=(
            P("section", "seq", None),
            P("section", "seq", None),
            P("section", None, "seq"),
            P("section", "seq"),
        ),
        check_vma=False,
    )
```

```python
import functools

import jax
import jax.numpy as jnp
from jax import lax
from jax.experimental import pallas as pl
from jax.experimental.pallas import tpu as pltpu
from jax.sharding import PartitionSpec as P

EPS = 1e-05
ROWS = 16
F32 = jnp.float32
BF16 = jnp.bfloat16


def dot(a, b, dims):
    return lax.dot_general(a, b, (dims, ((), ())), preferred_element_type=F32)


def to_row(column, rows):
    n = column.shape[0]
    return jnp.transpose(jnp.broadcast_to(column, (n, 128)))[:rows]


def to_col(row):
    n = row.shape[1]
    return jnp.transpose(jnp.broadcast_to(row, (128, n)))[:, :1]


def kernel(
    L, S, M, block,
    x_ref, gain_ref, w_ref, keep_ref, cot_ref,
    lo_ref, lg_ref, wg_ref, gg_ref,
    A, wp, raw, inv_ref, zout, g, zg, gs, tot, psend, prec, qsend, qrec, nsend, nrec, ggs, ggr,
    cot_sem, ag_sem, lo2_sem, n_sem, p_sem, q_sem, lg_sem, gg_sem, zf_sem, lo_sem, zb_sem,
):
    r = x_ref.shape[1]
    D = w_ref.shape[0]
    C = w_ref.shape[1]
    MB = S * r
    H = S // 2
    sec = lax.axis_index("section")
    me = lax.axis_index("seq")
    pair = me // 2
    par = me % 2
    partner = pair * 2 + 1 - par
    is_first = sec == 0
    is_last = sec == L - 1

    def col(i):
        return pl.ds(pl.multiple_of(i * C, C), C)

    def rows(i):
        return pl.ds(pl.multiple_of(i * r, r), r)

    def to(j):
        return (me + j) % S

    def fr(j):
        return (me + S - j) % S

    def mate(k):
        other, bit = pair, 1
        while bit < H:
            if k & bit:
                other = other + bit - 2 * bit * ((other // bit) % 2)
            bit *= 2
        return other * 2 + par

    relayed = H == 4
    direct = (1, 2) if relayed else tuple(range(1, H))
    near = 1 + par
    far = 2 - par

    def mate_of(k):
        return mate(1) * (2 - k) + mate(2) * (k - 1)

    def cp(src, dst, sem, idx, dev, section=None):
        return pltpu.make_async_remote_copy(
            src_ref=src,
            dst_ref=dst,
            send_sem=sem.at[(0,) + idx],
            recv_sem=sem.at[(1,) + idx],
            device_id=(sec if section is None else section, dev),
            device_id_type=pl.DeviceIdType.MESH,
        )

    def same(ref, sem, idx, dev, section=None):
        return cp(ref, ref, sem, idx, dev, section)

    others = range(1, S)
    mates = range(1, H)

    def cot_tx(m, j):
        d = to(j)
        return cp(cot_ref.at[m, :, col(d)], g.at[m, rows(me), :], cot_sem, (m, j), d)

    def cot_rx(m, j):
        f = fr(j)
        return same(g.at[m, rows(f), :], cot_sem, (m, j), f)

    def cols_of(m, i):
        return A.at[m, :, col(i)]

    def rows_of(m, i):
        return A.at[m, rows(i), :]

    def ag_tx(blk, m, k):
        return same(blk(m, me), ag_sem, (m, k), mate(k))

    def ag_rx(blk, m, k):
        return same(blk(m, mate(k)), ag_sem, (m, k), mate(k))

    def ag_near(blk, m):
        return same(blk(m, mate_of(near)), ag_sem, (m, near), mate_of(near))

    def ag_far(blk, m):
        return same(blk(m, mate_of(far)), ag_sem, (m, far), mate_of(far))

    def ag_relay_tx(blk, m):
        return same(blk(m, mate_of(near)), ag_sem, (m, 3), mate_of(far))

    def ag_relay_rx(blk, m):
        return same(blk(m, mate(3)), ag_sem, (m, 3), mate_of(far))

    def ag_ptx(blk, m):
        return same(blk(m, me), ag_sem, (m, 0), partner)

    def ag_prx(blk, m):
        return same(blk(m, partner), ag_sem, (m, 0), partner)

    def ag_ftx(blk, m, k):
        return same(blk(m, mate(k)), ag_sem, (m, H + k), partner)

    def ag_ftx_of(blk, m, k):
        return same(blk(m, mate_of(k)), ag_sem, (m, H + k), partner)

    def ag_frx(blk, m, k):
        return same(blk(m, mate(k) + 1 - 2 * par), ag_sem, (m, H + k), partner)

    def gather_start(blk, m):
        for k in direct:
            ag_tx(blk, m, k).start()
        ag_ptx(blk, m).start()

    def gather_pass(blk, m):
        if relayed:
            ag_near(blk, m).wait_recv()
            ag_relay_tx(blk, m).start()
            ag_ftx_of(blk, m, near).start()
            ag_far(blk, m).wait_recv()
            ag_ftx_of(blk, m, far).start()
        else:
            for k in direct:
                ag_rx(blk, m, k).wait_recv()
                ag_ftx(blk, m, k).start()

    def gather_last(blk, m):
        if relayed:
            ag_relay_rx(blk, m).wait_recv()
            ag_ftx(blk, m, 3).start()

    def gather_sent(blk, m):
        for k in direct:
            ag_tx(blk, m, k).wait_send()
        ag_ptx(blk, m).wait_send()
        if relayed:
            ag_relay_tx(blk, m).wait_send()
        for k in mates:
            ag_ftx(blk, m, k).wait_send()

    def zf_tx(m):
        return cp(zout.at[m], A.at[m, :, col(me)], zf_sem, (m,), me, sec + 1)

    def zf_rx(m):
        return same(A.at[m, :, col(me)], zf_sem, (m,), me, sec - 1)

    def lo_tx(m):
        return cp(A.at[m, rows(me), :], lo_ref.at[m], lo_sem, (m,), me, sec - 1)

    def lo_rx(m):
        return same(lo_ref.at[m], lo_sem, (m,), me, sec + 1)

    def lo2_tx(m, j):
        d = to(j)
        return cp(zout.at[m, rows(d), :], lo_ref.at[m, :, col(me)], lo2_sem, (m, j), d)

    def lo2_rx(m, j):
        f = fr(j)
        return same(lo_ref.at[m, :, col(f)], lo2_sem, (m, j), f)

    def n_tx(m, j):
        return cp(nsend.at[m], nrec.at[m, j], n_sem, (m, j), to(j))

    def n_rx(m, j):
        return same(nrec.at[m, j], n_sem, (m, j), fr(j))

    def p_tx(m, j):
        return cp(psend.at[m, j], prec.at[m, j], p_sem, (m, j), partner)

    def p_rx(m, j):
        return same(prec.at[m, j], p_sem, (m, j), partner)

    def q_tx(m, k):
        return cp(qsend.at[m, k], qrec.at[m, k], q_sem, (m, k), mate(k))

    def q_rx(m, k):
        return same(qrec.at[m, k], q_sem, (m, k), mate(k))

    def q_relay_tx(m):
        return cp(qsend.at[m, 3], qrec.at[m, 3], q_sem, (m, 3), mate_of(near))

    def q_relay_rx(m):
        return same(qrec.at[m, 3], q_sem, (m, 3), mate_of(near))

    def q_tx_of(m, k):
        return cp(qsend.at[m, k], qrec.at[m, k], q_sem, (m, k), mate_of(k))

    def zb_tx(m):
        return cp(zg.at[m], g.at[m], zb_sem, (m,), me, sec - 1)

    def zb_rx(m):
        return same(g.at[m], zb_sem, (m,), me, sec + 1)

    def lg_tx(m, j):
        d = to(j)
        return cp(zg.at[m, rows(d), :], lg_ref.at[m, :, col(me)], lg_sem, (m, j), d)

    def lg_rx(m, j):
        f = fr(j)
        return same(lg_ref.at[m, :, col(f)], lg_sem, (m, j), f)

    def gg_tx(j):
        d = to(j)
        return cp(ggs.at[d], ggr.at[j], gg_sem, (j,), d)

    def gg_rx(j):
        return same(ggr.at[j], gg_sem, (j,), fr(j))


    barrier = pltpu.get_barrier_semaphore()

    def greet(section, seq):
        pl.semaphore_signal(
            barrier, inc=1, device_id=(section, seq), device_id_type=pl.DeviceIdType.MESH
        )

    for j in others:
        greet(sec, to(j))

    @pl.when(sec > 0)
    def _():
        greet(sec - 1, me)

    @pl.when(sec < L - 1)
    def _():
        greet(sec + 1, me)

    neighbours = jnp.minimum(sec, 1) + jnp.minimum(L - 1 - sec, 1)
    pl.semaphore_wait(barrier, S - 1 + neighbours)

    @pl.when(is_first)
    def _():
        @pl.loop(0, M)
        def _(m):
            A[m, rows(me), :] = x_ref[m]
            gather_start(rows_of, m)

    @pl.when(is_last)
    def _():
        @pl.loop(0, M)
        def _(m):
            for j in others:
                cot_tx(m, j).start()
            g[m, rows(me), :] = cot_ref[m, :, col(me)]

    def keep_of(b):
        return jnp.broadcast_to(keep_ref[b][:, None, :], (C // block, block, C)).reshape(C, C)

    @pl.loop(0, S)
    def _(b):
        gain = to_col(gain_ref[:, col(b)])
        wp[col(b), :] = (w_ref[col(b), :].astype(F32) * gain * keep_of(b)).astype(BF16)

    def add_block(carry, m, b):
        acc, squares = carry
        part = A[m, :, col(b)]
        acc = acc + dot(part, wp[col(b), :], ((1,), (0,)))
        wide = part.astype(F32)
        return acc, squares + jnp.sum(wide * wide, axis=1, keepdims=True)

    def zero():
        return jnp.zeros((MB, C), F32), jnp.zeros((MB, 1), F32)

    def keep_sums(m, carry):
        raw[m] = carry[0]
        inv_ref[m] = jnp.broadcast_to(lax.rsqrt(carry[1] / D + EPS), (MB, 128))

    @pl.when(sec > 0)
    def _():
        zf_rx(0).wait_recv()
        gather_start(cols_of, 0)

    @pl.loop(0, M)
    def _(m):
        @pl.when(is_first)
        def _():
            gather_pass(rows_of, m)
            gather_last(rows_of, m)
            ag_prx(rows_of, m).wait_recv()
            for k in mates:
                ag_frx(rows_of, m, k).wait_recv()
            carry = zero()
            for b in range(S):
                carry = add_block(carry, m, b)
            keep_sums(m, carry)

        @pl.when(sec > 0)
        def _():
            carry = add_block(zero(), m, me)
            ag_prx(cols_of, m).wait_recv()
            carry = add_block(carry, m, partner)
            gather_pass(cols_of, m)
            for k in direct:
                carry = add_block(carry, m, mate(k))
                ag_frx(cols_of, m, k).wait_recv()
                carry = add_block(carry, m, mate(k) + 1 - 2 * par)
            gather_last(cols_of, m)

            @pl.when(m < M - 1)
            def _():
                zf_rx(m + 1).wait_recv()
                gather_start(cols_of, m + 1)

            if relayed:
                carry = add_block(carry, m, mate(3))
                ag_frx(cols_of, m, 3).wait_recv()
                carry = add_block(carry, m, mate(3) + 1 - 2 * par)
            keep_sums(m, carry)
            lo_tx(m).start()

        inv = inv_ref[m][:, :1]
        zout[m] = (A[m, :, col(me)].astype(F32) + inv * raw[m]).astype(BF16)

        @pl.when(sec < L - 1)
        def _():
            zf_tx(m).start()

        @pl.when(is_last)
        def _():
            for j in others:
                lo2_tx(m, j).start()
            lo_ref[m, :, col(me)] = zout[m, rows(me), :]

    def weight_grads():
        @pl.loop(0, S)
        def _(b):
            left = A[:, :, col(b)].reshape(M * MB, C)
            right = gs[...].reshape(M * MB, C)
            u = dot(left, right, ((0,), (0,))) * keep_of(b)
            wg_ref[col(b), :] = (u * to_col(gain_ref[:, col(b)])).astype(BF16)
            total = jnp.sum(u * w_ref[col(b), :].astype(F32), axis=1, keepdims=True)
            ggs[b] = to_row(total, 8)

        for j in others:
            gg_tx(j).start()

    def partial_of(m, b):
        return dot(g[m], wp[col(b), :], ((1,), (1,)))

    def spread(m):
        @pl.when(is_last)
        def _():
            for j in others:
                cot_rx(m, j).wait_recv()

        @pl.when(sec < L - 1)
        def _():
            zb_rx(m).wait_recv()

        order = [3, 1, 2, 0] if relayed else list(mates) + [0]
        for k in order:
            psend[m, k] = partial_of(m, mate(k) + 1 - 2 * par).astype(BF16)
            p_tx(m, k).start()

        def chip_sum(k, b):
            mine = partial_of(m, b)
            p_rx(m, k).wait_recv()
            return mine + prec[m, k].astype(F32)

        if relayed:
            qsend[m, 3] = chip_sum(3, mate(3)).astype(BF16)
            q_relay_tx(m).start()
            qsend[m, near] = chip_sum(near, mate_of(near)).astype(BF16)
            q_tx_of(m, near).start()
            last = chip_sum(far, mate_of(far))
            q_relay_rx(m).wait_recv()
            qsend[m, far] = (last + qrec[m, 3].astype(F32)).astype(BF16)
            q_tx_of(m, far).start()
        else:
            for k in mates:
                qsend[m, k] = chip_sum(k, mate(k)).astype(BF16)
                q_tx(m, k).start()
        gv = g[m].astype(F32)
        nsend[m] = to_row(jnp.sum(gv * raw[m], axis=1, keepdims=True), 8)
        for j in others:
            n_tx(m, j).start()
        gs[m] = (gv * inv_ref[m][:, :1]).astype(BF16)
        tot[m] = chip_sum(0, me)

    def lg_start(m):
        for j in others:
            lg_tx(m, j).start()

    def finish(m):
        scaled = tot[m]
        for k in direct:
            q_rx(m, k).wait_recv()
            scaled = scaled + qrec[m, k].astype(F32)
        for j in others:
            n_rx(m, j).wait_recv()
        sums = nsend[m]
        for j in others:
            sums = sums + nrec[m, j]
        inner = to_col(sums[:1]) / D
        inv = inv_ref[m][:, :1]
        grad = (
            g[m].astype(F32)
            + inv * scaled
            - A[m, :, col(me)].astype(F32) * (inv * inv * inv * inner)
        )
        zg[m] = grad.astype(BF16)

        @pl.when(sec > 0)
        def _():
            zb_tx(m).start()

        @pl.when(is_first)
        def _():
            lg_start(m)

        lg_ref[m, :, col(me)] = zg[m, rows(me), :]

    @pl.loop(0, M + 1)
    def _(i):
        @pl.when(i < M)
        def _():
            spread(i)

        @pl.when(i == M)
        def _():
            weight_grads()

        @pl.when(i > 0)
        def _():
            finish(i - 1)

    @pl.when(sec > 0)
    def _():
        @pl.loop(0, M)
        def _(m):
            lg_start(m)

    for j in others:
        gg_rx(j).wait_recv()
    sums = ggs[me]
    for j in others:
        sums = sums + ggr[j]
    gg_ref[...] = sums[:1]

    for j in others:
        gg_tx(j).wait_send()

    @pl.loop(0, M)
    def _(m):
        @pl.when(is_first)
        def _():
            gather_sent(rows_of, m)

        @pl.when(sec > 0)
        def _():
            gather_sent(cols_of, m)

        @pl.when(is_last)
        def _():
            for j in others:
                cot_tx(m, j).wait_send()
                lo2_tx(m, j).wait_send()
                lo2_rx(m, j).wait_recv()

        @pl.when(sec < L - 1)
        def _():
            zf_tx(m).wait_send()
            lo_rx(m).wait_recv()

        @pl.when(sec > 0)
        def _():
            lo_tx(m).wait_send()
            zb_tx(m).wait_send()

        for k in mates:
            q_tx(m, k).wait_send()
        for j in range(H):
            p_tx(m, j).wait_send()
        for j in others:
            n_tx(m, j).wait_send()
            lg_tx(m, j).wait_send()
            lg_rx(m, j).wait_recv()


def local(L, S, inputs, gains, weights, keep, cotangent):
    rows_dev, D = inputs.shape
    C = weights.shape[2]
    r = ROWS
    M = rows_dev // r
    MB = S * r
    H = S // 2
    block = D // keep.shape[1]
    keep_cols = jnp.repeat(keep[0].astype(F32), block, axis=1).reshape(S, C // block, C)
    vmem = pl.BlockSpec(memory_space=pltpu.VMEM)
    dma = pltpu.SemaphoreType.DMA
    lo, lg, wg, gg = pl.pallas_call(
        functools.partial(kernel, L, S, M, block),
        out_shape=(
            jax.ShapeDtypeStruct((M, r, D), BF16),
            jax.ShapeDtypeStruct((M, r, D), BF16),
            jax.ShapeDtypeStruct((D, C), BF16),
            jax.ShapeDtypeStruct((1, C), F32),
        ),
        in_specs=[vmem] * 5,
        out_specs=(vmem,) * 4,
        scratch_shapes=[
            pltpu.VMEM((M, MB, D), BF16),
            pltpu.VMEM((D, C), BF16),
            pltpu.VMEM((M, MB, C), F32),
            pltpu.VMEM((M, MB, 128), F32),
            pltpu.VMEM((M, MB, C), BF16),
            pltpu.VMEM((M, MB, C), BF16),
            pltpu.VMEM((M, MB, C), BF16),
            pltpu.VMEM((M, MB, C), BF16),
            pltpu.VMEM((M, MB, C), F32),
            pltpu.VMEM((M, H, MB, C), BF16),
            pltpu.VMEM((M, H, MB, C), BF16),
            pltpu.VMEM((M, H, MB, C), BF16),
            pltpu.VMEM((M, H, MB, C), BF16),
            pltpu.VMEM((M, 8, MB), F32),
            pltpu.VMEM((M, S, 8, MB), F32),
            pltpu.VMEM((S, 8, C), F32),
            pltpu.VMEM((S, 8, C), F32),
            dma((2, M, S)),
            dma((2, M, S)),
            dma((2, M, S)),
            dma((2, M, S)),
            dma((2, M, H)),
            dma((2, M, H)),
            dma((2, M, S)),
            dma((2, S)),
            dma((2, M)),
            dma((2, M)),
            dma((2, M)),
        ],
        compiler_params=pltpu.CompilerParams(
            collective_id=0, has_side_effects=True, vmem_limit_bytes=60 * 1024 * 1024
        ),
        cost_estimate=pl.CostEstimate(
            flops=6 * M * MB * D * C, bytes_accessed=12 * D * C, transcendentals=0
        ),
    )(
        inputs.reshape(M, r, D),
        gains,
        weights[0],
        keep_cols,
        cotangent.reshape(M, r, D),
    )
    return (
        lo.reshape(1, rows_dev, D),
        lg.reshape(1, rows_dev, D),
        wg[None],
        gg,
    )


def solution(mesh):
    placed = (
        P("seq", None),
        P("section", None),
        P("section", None, "seq"),
        P("section", None, "seq"),
        P("seq", None),
    )
    return jax.shard_map(
        functools.partial(local, mesh.shape["section"], mesh.shape["seq"]),
        mesh=mesh,
        in_specs=placed,
        out_specs=(
            P("section", "seq", None),
            P("section", "seq", None),
            P("section", None, "seq"),
            P("section", "seq"),
        ),
        check_vma=False,
    )
```
